256 devices in a mesh: blk: 64 (over y_hi, x, z), head: 4 (over y_lo, core).
Axes of the slice: x: 4, y: 4 (y_hi: 2, y_lo: 2; y = y_hi * 2 + y_lo), z: 8, core: 2. Of those that a mesh axis runs over, the one named last changes fastest.
Arguments:
- img_q: bfloat16 [32768, 3072], P(('blk', 'head')), may hold values from -60 to 60
- img_k: bfloat16 [32768, 3072], P(('blk', 'head')), may hold values from -20 to 20
- img_v: bfloat16 [32768, 3072], P(('blk', 'head')), may hold values from -6 to 6
- img_grad: bfloat16 [32768, 3072], P(('blk', 'head')), may hold values from -6 to 6
- txt_q: bfloat16 [256, 3072], P(None, 'head'), may hold values from -60 to 60
- txt_k: bfloat16 [256, 3072], P(None, 'head'), may hold values from -20 to 20
- txt_v: bfloat16 [256, 3072], P(None, 'head'), may hold values from -6 to 6
- txt_grad: bfloat16 [256, 3072], P(None, 'head'), may hold values from -6 to 6
Outputs:
- grad_img_q: bfloat16 [32768, 3072], P(('blk', 'head'))
- grad_img_k: bfloat16 [32768, 3072], P(('blk', 'head'))
- grad_img_v: bfloat16 [32768, 3072], P(('blk', 'head'))
- grad_txt_q: float32 [256, 3072], P(None, 'head')
- grad_txt_k: float32 [256, 3072], P(None, 'head')
- grad_txt_v: float32 [256, 3072], P(None, 'head')
The draws below stay inside these ranges and needn't reach their ends.
All inputs are finite; a program needn't handle non-finite values.
Results may differ from the reference program's by a relative error of at most 0.006.
Values may be sent and summed in bfloat16 or wider, within the bound.
A program may use at most 192 MiB of HBM per device.

```python
import jax
import jax.numpy as jnp
from jax import lax

HEADS = 24
HEAD_DIM = 128
TOK_BLK = 512
TXT = 256
BLOCKS = 64
IMG = 32768
D = 3072


def draw_img_k(key, part):
    key = jax.random.fold_in(key, 1)
    result = jnp.clip(jax.random.normal(key, (IMG, D), jnp.float32), -6.0, 6.0)
    return result.astype(jnp.bfloat16)


def draw_img_q(key, part):
    key = jax.random.fold_in(key, 2)
    result = jnp.clip(jax.random.normal(key, (IMG, D), jnp.float32), -6.0, 6.0)
    return result.astype(jnp.bfloat16)


def draw_txt_k(key, part):
    key = jax.random.fold_in(key, 3)
    result = jnp.clip(jax.random.normal(key, (TXT, D), jnp.float32), -6.0, 6.0)
    return result.astype(jnp.bfloat16)


def draw_txt_q(key, part):
    key = jax.random.fold_in(key, 4)
    result = jnp.clip(jax.random.normal(key, (TXT, D), jnp.float32), -6.0, 6.0)
    return result.astype(jnp.bfloat16)


def shard_levels(own_key, shape, split, low, top_value):
    loudness = 1.0
    for position, parts in split:
        heights = jax.random.uniform(jax.random.fold_in(jax.random.fold_in(own_key, 6), position), (parts,), jnp.float32, low / len(split), top_value / len(split))
        loudness = loudness * jnp.repeat(jnp.exp(heights), shape[position] // parts).reshape((-1,) + (1,) * (len(shape) - 1 - position))
    return loudness


def gaussian(stream_key, dims, deviation, most, shards=(), held_as=jnp.bfloat16):
    entries = deviation * jax.random.normal(stream_key, dims, jnp.float32)
    if shards:
        entries = entries * shard_levels(stream_key, dims, shards, -0.22, 0.18)
    return jnp.clip(entries, -most, most).astype(held_as)


def setup_inputs(seed: int = 0) -> dict:
    splits = jax.random.split(jax.random.key(seed), 9)
    return {
        "img_q": draw_img_q(jax.random.fold_in(splits[8], 71), 0),
        "img_k": draw_img_k(jax.random.fold_in(splits[8], 71), 0),
        "img_v": gaussian(splits[2], (IMG, D), 1.0, 6.0, ((0, 256),)),
        "img_grad": gaussian(splits[3], (IMG, D), 1.0, 6.0, ((0, 256),)),
        "txt_q": draw_txt_q(jax.random.fold_in(splits[8], 71), 0),
        "txt_k": draw_txt_k(jax.random.fold_in(splits[8], 71), 0),
        "txt_v": gaussian(splits[6], (TXT, D), 1.0, 6.0, ((1, 4),)),
        "txt_grad": gaussian(splits[7], (TXT, D), 1.0, 6.0, ((1, 4),)),
    }


def rows_grad(queries, grads, all_keys, all_values, scaling):
    scores = jnp.dot(queries, all_keys.T, preferred_element_type=jnp.float32) * scaling
    dprobs = jnp.dot(grads, all_values.T, preferred_element_type=jnp.float32)
    row_top = lax.optimization_barrier(jnp.max(scores, axis=1, keepdims=True))
    lifted = jnp.exp(scores - row_top)
    weights = lifted / lax.optimization_barrier(jnp.sum(lifted, axis=1, keepdims=True))
    row_delta = lax.optimization_barrier(jnp.sum(weights * dprobs, axis=1, keepdims=True))
    dscore = (weights * (dprobs - row_delta)).astype(jnp.bfloat16)
    probs_bf = weights.astype(jnp.bfloat16)
    grad_query = jnp.dot(dscore, all_keys, preferred_element_type=jnp.float32) * scaling
    grad_key = jnp.dot(dscore.T, queries, preferred_element_type=jnp.float32) * scaling
    grad_value = jnp.dot(probs_bf.T, grads, preferred_element_type=jnp.float32)
    return (grad_query, grad_key, grad_value)

def reference(img_q, img_k, img_v, img_grad, txt_q, txt_k, txt_v, txt_grad):
    scaling = HEAD_DIM ** (-0.5)

    def per_head(head_index):
        first_col = head_index * HEAD_DIM

        def head_slice(matrix):
            return lax.dynamic_slice_in_dim(matrix, first_col, HEAD_DIM, 1)
        image_query = head_slice(img_q)
        image_key = head_slice(img_k)
        image_value = head_slice(img_v)
        image_grad = head_slice(img_grad)
        text_query = head_slice(txt_q)
        text_key = head_slice(txt_k)
        text_value = head_slice(txt_v)
        text_grad = head_slice(txt_grad)
        text_dq, text_dk_all, text_dv_all = rows_grad(text_query, text_grad, jnp.concatenate([image_key, text_key], axis=0), jnp.concatenate([image_value, text_value], axis=0), scaling)
        block_query = image_query.reshape(BLOCKS, TOK_BLK, HEAD_DIM)
        block_grad = image_grad.reshape(BLOCKS, TOK_BLK, HEAD_DIM)
        block_key = image_key.reshape(BLOCKS, TOK_BLK, HEAD_DIM)
        block_value = image_value.reshape(BLOCKS, TOK_BLK, HEAD_DIM)
        prev_key = jnp.roll(block_key, 1, axis=0)
        prev_value = jnp.roll(block_value, 1, axis=0)

        def one_block(pieces):
            query_x, grad_x, key_x, value_x, prev_kx, prev_vx = pieces
            all_keys = jnp.concatenate([key_x, prev_kx, text_key], axis=0)
            all_values = jnp.concatenate([value_x, prev_vx, text_value], axis=0)
            grad_query, grad_key, grad_value = rows_grad(query_x, grad_x, all_keys, all_values, scaling)
            return (grad_query, grad_key[:TOK_BLK], grad_value[:TOK_BLK], grad_key[TOK_BLK:2 * TOK_BLK], grad_value[TOK_BLK:2 * TOK_BLK], grad_key[2 * TOK_BLK:], grad_value[2 * TOK_BLK:])
        outputs = lax.map(one_block, (block_query, block_grad, block_key, block_value, prev_key, prev_value))
        query_grad = outputs[0].reshape(IMG, HEAD_DIM)
        key_grad = (outputs[1] + jnp.roll(outputs[3], -1, axis=0)).reshape(IMG, HEAD_DIM) + text_dk_all[:IMG]
        value_grad = (outputs[2] + jnp.roll(outputs[4], -1, axis=0)).reshape(IMG, HEAD_DIM) + text_dv_all[:IMG]
        text_dk = text_dk_all[IMG:] + lax.optimization_barrier(jnp.sum(outputs[5], axis=0))
        text_dv = text_dv_all[IMG:] + lax.optimization_barrier(jnp.sum(outputs[6], axis=0))
        return (query_grad.astype(jnp.bfloat16), key_grad.astype(jnp.bfloat16), value_grad.astype(jnp.bfloat16), text_dq, text_dk, text_dv)
    results = lax.map(per_head, jnp.arange(HEADS, dtype=jnp.int32))

    def heads_joined(stack):
        return jnp.transpose(stack, (1, 0, 2)).reshape(stack.shape[1], HEADS * HEAD_DIM)
    return (heads_joined(results[0]), heads_joined(results[1]), heads_joined(results[2]), heads_joined(results[3]), heads_joined(results[4]), heads_joined(results[5]))
```

```python
import functools
import math

import jax
import jax.numpy as jnp
from jax import lax
from jax.experimental import pallas as pl
from jax.experimental.pallas import tpu as pltpu
from jax.sharding import PartitionSpec as P

HEAD_DIM = 128
SCALE = HEAD_DIM ** (-0.5)
EXP2_SCALE = SCALE * math.log2(math.e)
MESH = pl.DeviceIdType.MESH
F32 = jnp.float32
BF16 = jnp.bfloat16
STAT_ROWS = 8
VMEM_LIMIT = 50 * 1024 * 1024


def torus_sizes(blocks):
    return {64: (2, 4, 8), 8: (2, 2, 2), 4: (1, 2, 2)}[blocks]


class Place:
    def __init__(self, blocks, heads):
        self.blocks, self.heads = blocks, heads
        self.n_hi, self.n_x, self.n_z = torus_sizes(blocks)
        self.b = lax.axis_index("blk")
        self.c = lax.axis_index("head")
        self.z = lax.rem(self.b, self.n_z)
        self.x = lax.rem(self.b // self.n_z, self.n_x)
        self.hi = self.b // (self.n_z * self.n_x)

    def device(self, hi, x, z):
        return ((hi * self.n_x + x) * self.n_z + z, self.c)

    def next(self):
        return (lax.rem(self.b + 1, self.blocks), self.c)

    def prev(self):
        return (lax.rem(self.b + self.blocks - 1, self.blocks), self.c)

    def head_peer(self, step):
        return lax.rem(self.c + step, self.heads)

    def along_z(self, step):
        z = lax.rem(self.z + step, self.n_z)
        return z, self.device(self.hi, self.x, z)

    def along_x(self, step):
        x = lax.rem(self.x + step, self.n_x)
        return x, self.device(self.hi, x, self.z)

    def along_hi(self, step):
        return self.device(lax.rem(self.hi + step, self.n_hi), self.x, self.z)

    def in_plane(self, step):
        at = lax.rem(self.hi * self.n_x + self.x + step, self.n_hi * self.n_x)
        return self.device(at // self.n_x, lax.rem(at, self.n_x), self.z)


def meet(devices):
    barrier = pltpu.get_barrier_semaphore()
    for device in devices:
        pl.semaphore_signal(barrier, inc=1, device_id=device, device_id_type=MESH)
    pl.semaphore_wait(barrier, len(devices))


def remote(src, dst, sems, slot, device):
    return pltpu.make_async_remote_copy(
        src_ref=src,
        dst_ref=dst,
        send_sem=sems.at[(0,) + slot],
        recv_sem=sems.at[(1,) + slot],
        device_id=device,
        device_id_type=MESH,
    )


def dot_last(left, right):
    return lax.dot_general(
        left, right, (((1,), (1,)), ((), ())), preferred_element_type=F32
    )


def dot_plain(left, right):
    return lax.dot_general(
        left, right, (((1,), (0,)), ((), ())), preferred_element_type=F32
    )


def col_max(array):
    return jnp.max(array, axis=0, keepdims=True)


def col_sum(array):
    return jnp.sum(array, axis=0, keepdims=True)


def merge_stats(parts):
    top = functools.reduce(jnp.maximum, [p[0] for p in parts])
    total = jnp.zeros_like(top)
    dots = jnp.zeros_like(top)
    for part_top, part_total, part_dots in parts:
        factor = jnp.exp2(part_top - top)
        total += part_total * factor
        dots += part_dots * factor
    return top, total, dots


def split_stats(array):
    return tuple(array[i * STAT_ROWS : (i + 1) * STAT_ROWS] for i in range(3))


def gather_kernel(
    blocks, heads, img_q, img_k, img_v, img_g, txt_q, txt_k, txt_v, txt_g,
    q_all, k_all, v_all, g_all, k_prev, v_prev, stats,
    stat_z, stat_p, a2a_sems, own_sems, halo_sems, z_sems, p_sems,
):
    at = Place(blocks, heads)
    rows = img_q.shape[0]
    wide = q_all.shape[1]
    per_dev = wide // HEAD_DIM
    n_plane = at.n_hi * at.n_x
    meet(
        [(at.b, at.head_peer(s)) for s in range(1, heads)]
        + [at.next(), at.prev()]
        + [at.along_z(s)[1] for s in range(1, at.n_z)]
        + [at.in_plane(s) for s in range(1, n_plane)]
    )
    my_rows = pl.ds(at.c * rows, rows)
    arrays = [(img_k, k_all), (img_v, v_all), (img_q, q_all), (img_g, g_all)]
    sends = []
    for i, (src, dst) in enumerate(arrays):
        for s in range(1, heads):
            peer = at.head_peer(s)
            copy = remote(
                src.at[:, pl.ds(peer * wide, wide)],
                dst.at[my_rows, :],
                a2a_sems,
                (i, s),
                (at.b, peer),
            )
            copy.start()
            sends.append((i, copy))
        own = pltpu.make_async_copy(
            src.at[:, pl.ds(at.c * wide, wide)], dst.at[my_rows, :], own_sems.at[i]
        )
        own.start()
        sends.append((i, own))
    halo = []
    for i, dst in enumerate((k_prev, v_prev)):
        for j, copy in sends:
            if i == j:
                copy.wait()
        copy = remote(arrays[i][1], dst, halo_sems, (i,), at.next())
        copy.start()
        halo.append(copy)
    first = jnp.where(at.b == 0, 1.0, 0.0).astype(F32)
    stats[...] = jnp.zeros_like(stats)
    for h in range(per_dev):
        cols = pl.ds(h * HEAD_DIM, HEAD_DIM)
        query, grad = txt_q[:, cols], txt_g[:, cols]
        s_img = dot_last(k_all[:, cols], query) * EXP2_SCALE
        s_txt = dot_last(txt_k[:, cols], query) * EXP2_SCALE
        top = jnp.maximum(col_max(s_img), col_max(s_txt))
        p_img = jnp.exp2(s_img - top)
        p_txt = jnp.exp2(s_txt - top) * first
        d_img = dot_last(v_all[:, cols], grad)
        d_txt = dot_last(txt_v[:, cols], grad)
        stats[h : h + 1, :] = top
        stats[STAT_ROWS + h : STAT_ROWS + h + 1, :] = col_sum(p_img) + col_sum(p_txt)
        stats[2 * STAT_ROWS + h : 2 * STAT_ROWS + h + 1, :] = (
            col_sum(p_img * d_img) + col_sum(p_txt * d_txt)
        )
    stat_z[0] = stats[...]
    copies = []
    for s in range(1, at.n_z):
        copy = remote(stat_z.at[0], stat_z.at[s], z_sems, (s,), at.along_z(s)[1])
        copy.start()
        copies.append(copy)
    for copy in copies:
        copy.wait()
    merged = merge_stats([split_stats(stat_z[s]) for s in range(at.n_z)])
    for i in range(3):
        stat_p[0, i * STAT_ROWS : (i + 1) * STAT_ROWS, :] = merged[i]
    copies = []
    for s in range(1, n_plane):
        copy = remote(stat_p.at[0], stat_p.at[s], p_sems, (s,), at.in_plane(s))
        copy.start()
        copies.append(copy)
    for copy in copies:
        copy.wait()
    merged = merge_stats([split_stats(stat_p[s]) for s in range(n_plane)])
    for i in range(3):
        stats[i * STAT_ROWS : (i + 1) * STAT_ROWS, :] = merged[i]
    for copy in halo:
        copy.wait()
    for i, copy in sends:
        if i >= 2:
            copy.wait()


def attention_kernel(
    blocks, q, k, v, g, kp, vp, tq, tk, tv, tg, stats,
    dq, dko, dvo, dkp, dvp, dtq, dtk, dtv,
):
    h = pl.program_id(0)
    first = jnp.where(lax.axis_index("blk") == 0, 1.0, 0.0).astype(F32)
    query, grad = tq[...], tg[...]
    top = stats[pl.ds(h, 1), :]
    total = stats[pl.ds(STAT_ROWS + h, 1), :]
    delta = stats[pl.ds(2 * STAT_ROWS + h, 1), :] / total
    inverse = 1.0 / total
    w_img = jnp.exp2(dot_last(k[...], query) * EXP2_SCALE - top) * inverse
    ds_img = (w_img * (dot_last(v[...], grad) - delta)).astype(BF16)
    w_txt = jnp.exp2(dot_last(tk[...], query) * EXP2_SCALE - top) * (inverse * first)
    ds_txt = (w_txt * (dot_last(tv[...], grad) - delta)).astype(BF16)
    k_t, tk_t = k[...].T, tk[...].T
    dtq[...] = (dot_plain(k_t, ds_img) + dot_plain(tk_t, ds_txt)).T * SCALE
    dko[...] = dot_plain(ds_img, query)
    dvo[...] = dot_plain(w_img.astype(BF16), grad)
    dtk[...] = dot_plain(ds_txt, query)
    dtv[...] = dot_plain(w_txt.astype(BF16), grad)
    kp_t = kp[...].T
    keys = [k, kp, tk]
    values = [v, vp, tv]
    tile = 256
    dk_parts, dv_parts = [None] * 3, [None] * 3
    for r in range(0, q.shape[0], tile):
        query, grad = q[r : r + tile, :], g[r : r + tile, :]
        scores = [dot_last(key[...], query) for key in keys]
        top = functools.reduce(jnp.maximum, [col_max(s) for s in scores]) * EXP2_SCALE
        lifted = [jnp.exp2(s * EXP2_SCALE - top) for s in scores]
        dprobs = [dot_last(value[...], grad) for value in values]
        total = sum(col_sum(p) for p in lifted)
        inverse = 1.0 / total
        delta = sum(col_sum(p * d) for p, d in zip(lifted, dprobs)) * inverse
        query_part = None
        for i, key_t in enumerate((k_t, kp_t, tk_t)):
            weights = lifted[i] * inverse
            dscore = (weights * (dprobs[i] - delta)).astype(BF16)
            dk = dot_plain(dscore, query)
            dv = dot_plain(weights.astype(BF16), grad)
            dk_parts[i] = dk if r == 0 else dk_parts[i] + dk
            dv_parts[i] = dv if r == 0 else dv_parts[i] + dv
            part = dot_plain(key_t, dscore)
            query_part = part if query_part is None else query_part + part
        dq[r : r + tile, :] = (query_part.T * SCALE).astype(BF16)
    dko[...] = (dko[...] + dk_parts[0]) * SCALE
    dvo[...] = dvo[...] + dv_parts[0]
    dkp[...] = (dk_parts[1] * SCALE).astype(BF16)
    dvp[...] = dv_parts[1].astype(BF16)
    dtk[...] = (dtk[...] + dk_parts[2]) * SCALE
    dtv[...] = dtv[...] + dv_parts[2]


def return_kernel(
    blocks, heads, dq, dko, dvo, dkp, dvp, dtq, dtk, dtv,
    out_q, out_k, out_v, out_tq, out_tk, out_tv,
    back, ready, part, part16, x_in, x_sum, x_sum16, z_in, hi_in, z_all, x_all,
    a2a_sems, own_sems, back_sems, x_sems, z_sems, hi_sems, zg_sems, xg_sems,
):
    at = Place(blocks, heads)
    rows = out_q.shape[0]
    wide = dq.shape[1]
    per_dev = wide // HEAD_DIM
    txt = dtq.shape[0]
    meet(
        [(at.b, at.head_peer(s)) for s in range(1, heads)]
        + [at.next(), at.prev()]
        + [at.along_z(s)[1] for s in range(1, at.n_z)]
        + [at.along_x(s)[1] for s in range(1, at.n_x)]
        + [at.along_hi(s) for s in range(1, at.n_hi)]
    )
    my_cols = pl.ds(at.c * wide, wide)

    def hand_out(i, src, dst):
        copies = []
        for s in range(1, heads):
            peer = at.head_peer(s)
            copies.append(
                remote(
                    src.at[pl.ds(peer * rows, rows), :],
                    dst.at[:, my_cols],
                    a2a_sems,
                    (i, s),
                    (at.b, peer),
                )
            )
        copies.append(
            pltpu.make_async_copy(
                src.at[pl.ds(at.c * rows, rows), :], dst.at[:, my_cols], own_sems.at[i]
            )
        )
        for copy in copies:
            copy.start()
        return copies

    returned = []
    for i, src in enumerate((dkp, dvp)):
        copy = remote(src, back.at[i], back_sems, (i,), at.prev())
        copy.start()
        returned.append(copy)
    out_copies = hand_out(0, dq, out_q)

    for i, src in enumerate((dtq, dtk, dtv)):
        for h in range(per_dev):
            piece = pl.ds((i * per_dev + h) * txt, txt)
            value = src[:, h * HEAD_DIM : (h + 1) * HEAD_DIM]
            part[piece, :] = value
            part16[piece, :] = value.astype(BF16)
    n_xr = part.shape[0] // at.n_x
    n_zr = n_xr // at.n_z
    copies = []
    for s in range(1, at.n_x):
        x, device = at.along_x(s)
        copies.append(
            remote(part16.at[pl.ds(x * n_xr, n_xr), :], x_in.at[s - 1], x_sems, (s,), device)
        )
        copies[-1].start()
    for copy in copies:
        copy.wait()
    value = part[pl.ds(at.x * n_xr, n_xr), :]
    for s in range(1, at.n_x):
        value = value + x_in[s - 1].astype(F32)
    x_sum[...] = value
    x_sum16[...] = value.astype(BF16)
    copies = []
    for s in range(1, at.n_z):
        z, device = at.along_z(s)
        copies.append(
            remote(x_sum16.at[pl.ds(z * n_zr, n_zr), :], z_in.at[s - 1], z_sems, (s,), device)
        )
        copies[-1].start()

    for i, (src, dst) in enumerate(((dko, out_k), (dvo, out_v))):
        returned[i].wait()
        ready[i] = (src[...] + back[i].astype(F32)).astype(BF16)
        out_copies += hand_out(i + 1, ready.at[i], dst)

    for copy in copies:
        copy.wait()
    value = x_sum[pl.ds(at.z * n_zr, n_zr), :]
    for s in range(1, at.n_z):
        value = value + z_in[s - 1].astype(F32)
    hi_in[0] = value
    for s in range(1, at.n_hi):
        copy = remote(hi_in.at[0], hi_in.at[s], hi_sems, (s,), at.along_hi(s))
        copy.start()
        copy.wait()
        value = value + hi_in[s]
    mine = pl.ds(at.z * n_zr, n_zr)
    z_all[mine, :] = value.astype(BF16)
    copies = []
    for s in range(1, at.n_z):
        copies.append(
            remote(z_all.at[mine, :], z_all.at[mine, :], zg_sems, (s,), at.along_z(s)[1])
        )
        copies[-1].start()
    for copy in copies:
        copy.wait()
    mine = pl.ds(at.x * n_xr, n_xr)
    x_all[mine, :] = z_all[...]
    copies = []
    for s in range(1, at.n_x):
        copies.append(
            remote(z_all, x_all.at[mine, :], xg_sems, (s,), at.along_x(s)[1])
        )
        copies[-1].start()
    for copy in copies:
        copy.wait()
    for i, dst in enumerate((out_tq, out_tk, out_tv)):
        for h in range(per_dev):
            piece = pl.ds((i * per_dev + h) * txt, txt)
            dst[:, h * HEAD_DIM : (h + 1) * HEAD_DIM] = x_all[piece, :].astype(F32)
    for copy in out_copies:
        copy.wait()


def dma(*shape):
    return pltpu.SemaphoreType.DMA(shape)


def body(blocks, heads, img_q, img_k, img_v, img_g, txt_q, txt_k, txt_v, txt_g):
    n_hi, n_x, n_z = torus_sizes(blocks)
    rows, width = img_q.shape
    txt, wide = txt_q.shape
    block_rows = rows * heads
    per_dev = wide // HEAD_DIM
    in_vmem = pl.BlockSpec(memory_space=pltpu.VMEM)
    anywhere = pl.BlockSpec(memory_space=pl.ANY)
    block16 = jax.ShapeDtypeStruct((block_rows, wide), BF16)
    block32 = jax.ShapeDtypeStruct((block_rows, wide), F32)
    stat_shape = (3 * STAT_ROWS, txt)
    gathered = pl.pallas_call(
        functools.partial(gather_kernel, blocks, heads),
        out_shape=[block16] * 6 + [jax.ShapeDtypeStruct(stat_shape, F32)],
        in_specs=[anywhere] * 4 + [in_vmem] * 4,
        out_specs=[in_vmem] * 7,
        scratch_shapes=[
            pltpu.VMEM((n_z,) + stat_shape, F32),
            pltpu.VMEM((n_hi * n_x,) + stat_shape, F32),
            dma(2, 4, heads),
            dma(4),
            dma(2, 2),
            dma(2, n_z),
            dma(2, n_hi * n_x),
        ],
        compiler_params=pltpu.CompilerParams(
            collective_id=0, has_side_effects=True, vmem_limit_bytes=VMEM_LIMIT
        ),
        name="gather_rows",
    )(img_q, img_k, img_v, img_g, txt_q, txt_k, txt_v, txt_g)
    block_spec = pl.BlockSpec((block_rows, HEAD_DIM), lambda h: (0, h))
    text_spec = pl.BlockSpec((txt, HEAD_DIM), lambda h: (0, h))
    text32 = jax.ShapeDtypeStruct((txt, wide), F32)
    grads = pl.pallas_call(
        functools.partial(attention_kernel, blocks),
        grid=(per_dev,),
        out_shape=[block16, block32, block32, block16, block16] + [text32] * 3,
        in_specs=[block_spec] * 6
        + [text_spec] * 4
        + [pl.BlockSpec(stat_shape, lambda h: (0, 0))],
        out_specs=[block_spec] * 5 + [text_spec] * 3,
        compiler_params=pltpu.CompilerParams(vmem_limit_bytes=VMEM_LIMIT),
        name="attention_grads",
    )(*gathered[:6], txt_q, txt_k, txt_v, txt_g, gathered[6])
    n_rows = 3 * per_dev * txt
    x_rows = n_rows // n_x
    z_rows = x_rows // n_z
    out16 = jax.ShapeDtypeStruct((rows, width), BF16)
    return tuple(
        pl.pallas_call(
            functools.partial(return_kernel, blocks, heads),
            out_shape=[out16] * 3 + [text32] * 3,
            in_specs=[in_vmem] * 8,
            out_specs=[anywhere] * 3 + [in_vmem] * 3,
            scratch_shapes=[
                pltpu.VMEM((2, block_rows, wide), BF16),
                pltpu.VMEM((2, block_rows, wide), BF16),
                pltpu.VMEM((n_rows, HEAD_DIM), F32),
                pltpu.VMEM((n_rows, HEAD_DIM), BF16),
                pltpu.VMEM((n_x - 1, x_rows, HEAD_DIM), BF16),
                pltpu.VMEM((x_rows, HEAD_DIM), F32),
                pltpu.VMEM((x_rows, HEAD_DIM), BF16),
                pltpu.VMEM((n_z - 1, z_rows, HEAD_DIM), BF16),
                pltpu.VMEM((n_hi, z_rows, HEAD_DIM), F32),
                pltpu.VMEM((x_rows, HEAD_DIM), BF16),
                pltpu.VMEM((n_rows, HEAD_DIM), BF16),
                dma(2, 3, heads),
                dma(3),
                dma(2, 2),
                dma(2, n_x),
                dma(2, n_z),
                dma(2, n_hi),
                dma(2, n_z),
                dma(2, n_x),
            ],
            compiler_params=pltpu.CompilerParams(
                collective_id=1, has_side_effects=True, vmem_limit_bytes=VMEM_LIMIT
            ),
            name="return_rows",
        )(*grads)
    )


def solution(mesh):
    rows = P(("blk", "head"), None)
    text = P(None, "head")
    return jax.shard_map(
        functools.partial(body, mesh.shape["blk"], mesh.shape["head"]),
        mesh=mesh,
        in_specs=(rows,) * 4 + (text,) * 4,
        out_specs=(rows,) * 3 + (text,) * 3,
        check_vma=False,
    )
```

```python
import functools
import math
from types import SimpleNamespace

import jax
import jax.numpy as jnp
from jax import lax
from jax.experimental import pallas as pl
from jax.experimental.pallas import tpu as pltpu
from jax.sharding import PartitionSpec as P

HEAD_DIM = 128
SCALE = HEAD_DIM ** (-0.5)
EXP2_SCALE = SCALE * math.log2(math.e)
MESH = pl.DeviceIdType.MESH
F32 = jnp.float32
BF16 = jnp.bfloat16
STAT_ROWS = 8
GROUP = 2
LEAD = 3
TILE = 256
VMEM_LIMIT = 50 * 1024 * 1024


def torus_sizes(blocks):
    return {64: (2, 4, 8), 8: (2, 2, 2), 4: (1, 2, 2)}[blocks]


class Place:
    def __init__(self, blocks, heads):
        self.blocks, self.heads = blocks, heads
        self.n_hi, self.n_x, self.n_z = torus_sizes(blocks)
        self.b = lax.axis_index("blk")
        self.c = lax.axis_index("head")
        self.z = lax.rem(self.b, self.n_z)
        self.x = lax.rem(self.b // self.n_z, self.n_x)
        self.hi = self.b // (self.n_z * self.n_x)

    def device(self, hi, x, z):
        return ((hi * self.n_x + x) * self.n_z + z, self.c)

    def next(self):
        return (lax.rem(self.b + 1, self.blocks), self.c)

    def prev(self):
        return (lax.rem(self.b + self.blocks - 1, self.blocks), self.c)

    def head_peer(self, step):
        return lax.rem(self.c + step, self.heads)

    def along_z(self, step):
        z = lax.rem(self.z + step, self.n_z)
        return z, self.device(self.hi, self.x, z)

    def along_x(self, step):
        x = lax.rem(self.x + step, self.n_x)
        return x, self.device(self.hi, x, self.z)

    def along_hi(self, step):
        return self.device(lax.rem(self.hi + step, self.n_hi), self.x, self.z)

    def in_plane(self, step):
        at = lax.rem(self.hi * self.n_x + self.x + step, self.n_hi * self.n_x)
        return self.device(at // self.n_x, lax.rem(at, self.n_x), self.z)


def meet(devices):
    barrier = pltpu.get_barrier_semaphore()
    for device in devices:
        pl.semaphore_signal(barrier, inc=1, device_id=device, device_id_type=MESH)
    pl.semaphore_wait(barrier, len(devices))


def remote(src, dst, sems, slot, device):
    return pltpu.make_async_remote_copy(
        src_ref=src,
        dst_ref=dst,
        send_sem=sems.at[(0,) + slot],
        recv_sem=sems.at[(1,) + slot],
        device_id=device,
        device_id_type=MESH,
    )


def dot_last(left, right):
    return lax.dot_general(
        left, right, (((1,), (1,)), ((), ())), preferred_element_type=F32
    )


def dot_plain(left, right):
    return lax.dot_general(
        left, right, (((1,), (0,)), ((), ())), preferred_element_type=F32
    )


def col_max(array):
    return jnp.max(array, axis=0, keepdims=True)


def col_sum(array):
    return jnp.sum(array, axis=0, keepdims=True)


def merge_stats(parts, per_group):
    rows = [[p[i * per_group : (i + 1) * per_group] for i in range(3)] for p in parts]
    top = functools.reduce(jnp.maximum, [r[0] for r in rows])
    total = jnp.zeros_like(top)
    dots = jnp.zeros_like(top)
    for part_top, part_total, part_dots in rows:
        factor = jnp.exp2(part_top - top)
        total += part_total * factor
        dots += part_dots * factor
    return top, total, dots


def dma(*shape):
    return pltpu.SemaphoreType.DMA(shape)


def scratch(blocks, heads, rows, wide, txt):
    n_hi, n_x, n_z = torus_sizes(blocks)
    plane = n_hi * n_x
    n = wide // HEAD_DIM
    groups = n // GROUP
    block = rows * heads
    sums = 3 * GROUP * txt
    xr = sums // n_x
    zr = xr // n_z
    d = HEAD_DIM
    return dict(
        text=pltpu.VMEM((4, txt, wide), BF16),
        landed=pltpu.VMEM((4, n, block, d), BF16),
        halo=pltpu.VMEM((2, n, block, d), BF16),
        ready=pltpu.VMEM((3, n, block, d), BF16),
        own=pltpu.VMEM((2, n, block, d), F32),
        give=pltpu.VMEM((2, n, block, d), BF16),
        back=pltpu.VMEM((2, n, block, d), BF16),
        stat_z=pltpu.VMEM((groups, n_z, STAT_ROWS, txt), F32),
        stat_p=pltpu.VMEM((groups, plane, STAT_ROWS, txt), F32),
        stat=pltpu.VMEM((groups, STAT_ROWS, txt), F32),
        part=pltpu.VMEM((groups, sums, d), F32),
        part16=pltpu.VMEM((groups, sums, d), BF16),
        x_in=pltpu.VMEM((groups, n_x - 1, xr, d), BF16),
        x_sum=pltpu.VMEM((groups, xr, d), F32),
        x_sum16=pltpu.VMEM((groups, xr, d), BF16),
        z_in=pltpu.VMEM((groups, n_z - 1, zr, d), BF16),
        hi_in=pltpu.VMEM((groups, n_hi, zr, d), F32),
        z_all=pltpu.VMEM((groups, xr, d), BF16),
        x_all=pltpu.VMEM((groups, sums, d), BF16),
        text_sems=dma(4),
        in_sems=dma(2, n, 4, heads),
        in_own=dma(n, 4),
        halo_sems=dma(2, n, 2),
        back_sems=dma(2, n, 2),
        out_sems=dma(2, n, 3, heads),
        out_own=dma(n, 3),
        sz_sems=dma(2, groups, n_z),
        sp_sems=dma(2, groups, plane),
        xs_sems=dma(2, groups, n_x),
        zs_sems=dma(2, groups, n_z),
        hi_sems=dma(2, groups, n_hi),
        zg_sems=dma(2, groups, n_z),
        xg_sems=dma(2, groups, n_x),
    )


def kernel(blocks, heads, names, *refs):
    ins, outs, rest = refs[:8], refs[8:14], refs[14:]
    images, texts = ins[:4], ins[4:]
    m = SimpleNamespace(**dict(zip(names, rest)))
    at = Place(blocks, heads)
    rows = outs[0].shape[0]
    txt, wide = outs[3].shape
    n = wide // HEAD_DIM
    groups = n // GROUP
    plane = at.n_hi * at.n_x
    xr, zr = m.x_sum.shape[1], m.z_in.shape[2]
    block = rows * heads
    my_rows = pl.ds(at.c * rows, rows)
    first = jnp.where(at.b == 0, 1.0, 0.0).astype(F32)

    def head_cols(owner, h):
        return pl.ds(pl.multiple_of(owner * wide + h * HEAD_DIM, HEAD_DIM), HEAD_DIM)


    def arrive(h, i, s):
        peer = at.head_peer(s)
        return remote(
            images[i].at[:, head_cols(peer, h)],
            m.landed.at[i, h, my_rows, :],
            m.in_sems, (h, i, s), (at.b, peer),
        )

    def arrive_own(h, i):
        return pltpu.make_async_copy(
            images[i].at[:, head_cols(at.c, h)],
            m.landed.at[i, h, my_rows, :],
            m.in_own.at[h, i],
        )

    def halo(h, i):
        return remote(
            m.landed.at[i + 1, h], m.halo.at[i, h], m.halo_sems, (h, i), at.next()
        )

    def give_back(h, i):
        return remote(m.give.at[i, h], m.back.at[i, h], m.back_sems, (h, i), at.prev())

    def leave(h, i, s):
        peer = at.head_peer(s)
        return remote(
            m.ready.at[i, h, pl.ds(peer * rows, rows), :],
            outs[i].at[:, head_cols(at.c, h)],
            m.out_sems, (h, i, s), (at.b, peer),
        )

    def leave_own(h, i):
        return pltpu.make_async_copy(
            m.ready.at[i, h, my_rows, :],
            outs[i].at[:, head_cols(at.c, h)],
            m.out_own.at[h, i],
        )

    def stats_z(g, s):
        return remote(
            m.stat_z.at[g, 0], m.stat_z.at[g, s], m.sz_sems, (g, s), at.along_z(s)[1]
        )

    def stats_p(g, s):
        return remote(
            m.stat_p.at[g, 0], m.stat_p.at[g, s], m.sp_sems, (g, s), at.in_plane(s)
        )

    def scatter_x(g, s):
        x, device = at.along_x(s)
        return remote(
            m.part16.at[g, pl.ds(x * xr, xr), :], m.x_in.at[g, s - 1],
            m.xs_sems, (g, s), device,
        )

    def scatter_z(g, s):
        z, device = at.along_z(s)
        return remote(
            m.x_sum16.at[g, pl.ds(z * zr, zr), :], m.z_in.at[g, s - 1],
            m.zs_sems, (g, s), device,
        )

    def swap_hi(g, s):
        return remote(
            m.hi_in.at[g, 0], m.hi_in.at[g, s], m.hi_sems, (g, s), at.along_hi(s)
        )

    my_z = pl.ds(at.z * zr, zr)
    my_x = pl.ds(at.x * xr, xr)

    def gather_z(g, s):
        return remote(
            m.z_all.at[g, my_z, :], m.z_all.at[g, my_z, :],
            m.zg_sems, (g, s), at.along_z(s)[1],
        )

    def gather_x(g, s):
        return remote(
            m.z_all.at[g], m.x_all.at[g, my_x, :],
            m.xg_sems, (g, s), at.along_x(s)[1],
        )

    group_moves = [
        (stats_z, at.n_z), (stats_p, plane), (scatter_x, at.n_x), (scatter_z, at.n_z),
        (swap_hi, at.n_hi), (gather_z, at.n_z), (gather_x, at.n_x),
    ]

    def start_all(move, count, g):
        for s in range(1, count):
            move(g, s).start()

    def await_all(move, count, g):
        for s in range(1, count):
            move(g, s).wait_recv()


    def send_in(h):
        for i in (1, 2, 0, 3):
            for s in (2, 3, 1) if heads == 4 else range(1, heads):
                arrive(h, i, s).start()
            arrive_own(h, i).start()

    def await_in(h, i):
        for s in range(1, heads):
            arrive(h, i, s).wait_recv()
        arrive_own(h, i).wait()

    def send_out(h, i):
        for s in (2, 3, 1) if heads == 4 else range(1, heads):
            leave(h, i, s).start()
        leave_own(h, i).start()

    def text_rows(i, h):
        return m.text[i, :, pl.ds(pl.multiple_of(h * HEAD_DIM, HEAD_DIM), HEAD_DIM)]

    def keys_in(h):
        for i in (1, 2):
            await_in(h, i)
            halo(h, i - 1).start()
        g, hh = h // GROUP, lax.rem(h, GROUP)
        query, grad = text_rows(0, h), text_rows(3, h)
        s_img = dot_last(m.landed[1, h], query) * EXP2_SCALE
        s_txt = dot_last(text_rows(1, h), query) * EXP2_SCALE
        top = jnp.maximum(col_max(s_img), col_max(s_txt))
        p_img = jnp.exp2(s_img - top)
        p_txt = jnp.exp2(s_txt - top) * first
        d_img = dot_last(m.landed[2, h], grad)
        d_txt = dot_last(text_rows(2, h), grad)
        m.stat_z[g, 0, pl.ds(hh, 1), :] = top
        m.stat_z[g, 0, pl.ds(GROUP + hh, 1), :] = col_sum(p_img) + col_sum(p_txt)
        m.stat_z[g, 0, pl.ds(2 * GROUP + hh, 1), :] = col_sum(p_img * d_img) + col_sum(
            p_txt * d_txt
        )

    def merge_z(g):
        await_all(stats_z, at.n_z, g)
        merged = merge_stats([m.stat_z[g, s] for s in range(at.n_z)], GROUP)
        m.stat_p[g, 0] = jnp.zeros_like(m.stat_p[g, 0])
        for i in range(3):
            m.stat_p[g, 0, i * GROUP : (i + 1) * GROUP, :] = merged[i]
        start_all(stats_p, plane, g)

    def merge_plane(g):
        await_all(stats_p, plane, g)
        merged = merge_stats([m.stat_p[g, s] for s in range(plane)], GROUP)
        for i in range(3):
            m.stat[g, i * GROUP : (i + 1) * GROUP, :] = merged[i]

    def part_rows(i, hh):
        return pl.ds(pl.multiple_of((i * GROUP + hh) * txt, txt), txt)

    def text_grads(g, hh):
        h = g * GROUP + hh
        query, grad = text_rows(0, h), text_rows(3, h)
        key, value = m.landed[1, h], m.landed[2, h]
        text_key, text_value = text_rows(1, h), text_rows(2, h)
        top = m.stat[g, pl.ds(hh, 1), :]
        total = m.stat[g, pl.ds(GROUP + hh, 1), :]
        inverse = 1.0 / total
        delta = m.stat[g, pl.ds(2 * GROUP + hh, 1), :] * inverse
        w_img = jnp.exp2(dot_last(key, query) * EXP2_SCALE - top) * inverse
        ds_img = (w_img * (dot_last(value, grad) - delta)).astype(BF16)
        w_txt = jnp.exp2(dot_last(text_key, query) * EXP2_SCALE - top) * (inverse * first)
        ds_txt = (w_txt * (dot_last(text_value, grad) - delta)).astype(BF16)
        m.own[0, h] += dot_plain(ds_img, query) * SCALE
        m.own[1, h] += dot_plain(w_img.astype(BF16), grad)
        sums = [
            (dot_plain(key.T, ds_img) + dot_plain(text_key.T, ds_txt)).T * SCALE,
            m.part[g, part_rows(1, hh), :] + dot_plain(ds_txt, query) * SCALE,
            m.part[g, part_rows(2, hh), :] + dot_plain(w_txt.astype(BF16), grad),
        ]
        for i in range(3):
            m.part[g, part_rows(i, hh), :] = sums[i]
            m.part16[g, part_rows(i, hh), :] = sums[i].astype(BF16)

    def image_grads(h):
        for i in (0, 3):
            await_in(h, i)
        for i in range(2):
            halo(h, i).wait_recv()
        g, hh = h // GROUP, lax.rem(h, GROUP)
        keys = [m.landed[1, h], m.halo[0, h], text_rows(1, h)]
        values = [m.landed[2, h], m.halo[1, h], text_rows(2, h)]
        turned = [key.T for key in keys]
        dk_parts, dv_parts = [None] * 3, [None] * 3
        for r in range(0, block, min(block, TILE)):
            these = slice(r, r + min(block, TILE))
            query, grad = m.landed[0, h, these, :], m.landed[3, h, these, :]
            scores = [dot_last(key, query) for key in keys]
            top = functools.reduce(jnp.maximum, [col_max(s) for s in scores]) * EXP2_SCALE
            lifted = [jnp.exp2(s * EXP2_SCALE - top) for s in scores]
            dprobs = [dot_last(value, grad) for value in values]
            inverse = 1.0 / sum(col_sum(p) for p in lifted)
            delta = sum(col_sum(p * d) for p, d in zip(lifted, dprobs)) * inverse
            query_part = None
            for i in range(3):
                weights = lifted[i] * inverse
                dscore = (weights * (dprobs[i] - delta)).astype(BF16)
                dk = dot_plain(dscore, query)
                dv = dot_plain(weights.astype(BF16), grad)
                dk_parts[i] = dk if r == 0 else dk_parts[i] + dk
                dv_parts[i] = dv if r == 0 else dv_parts[i] + dv
                part = dot_plain(turned[i], dscore)
                query_part = part if query_part is None else query_part + part
            m.ready[0, h, these, :] = (query_part.T * SCALE).astype(BF16)
        m.give[0, h] = (dk_parts[1] * SCALE).astype(BF16)
        m.give[1, h] = dv_parts[1].astype(BF16)
        for i in range(2):
            give_back(h, i).start()
        send_out(h, 0)
        m.own[0, h] = dk_parts[0] * SCALE
        m.own[1, h] = dv_parts[0]
        m.part[g, part_rows(1, hh), :] = dk_parts[2] * SCALE
        m.part[g, part_rows(2, hh), :] = dv_parts[2]

    def finish(h):
        for i in range(2):
            give_back(h, i).wait_recv()
            m.ready[i + 1, h] = (m.own[i, h] + m.back[i, h].astype(F32)).astype(BF16)
            send_out(h, i + 1)

    def sum_x(g):
        await_all(scatter_x, at.n_x, g)
        value = m.part[g, my_x, :]
        for s in range(1, at.n_x):
            value = value + m.x_in[g, s - 1].astype(F32)
        m.x_sum[g] = value
        m.x_sum16[g] = value.astype(BF16)
        start_all(scatter_z, at.n_z, g)

    def sum_z(g):
        await_all(scatter_z, at.n_z, g)
        value = m.x_sum[g, my_z, :]
        for s in range(1, at.n_z):
            value = value + m.z_in[g, s - 1].astype(F32)
        m.hi_in[g, 0] = value
        start_all(swap_hi, at.n_hi, g)

    def sum_hi(g):
        await_all(swap_hi, at.n_hi, g)
        value = m.hi_in[g, 0]
        for s in range(1, at.n_hi):
            value = value + m.hi_in[g, s]
        m.z_all[g, my_z, :] = value.astype(BF16)
        start_all(gather_z, at.n_z, g)

    def spread(g):
        await_all(gather_z, at.n_z, g)
        m.x_all[g, my_x, :] = m.z_all[g]
        start_all(gather_x, at.n_x, g)

    def write_text(g):
        await_all(gather_x, at.n_x, g)
        for i in range(3):
            for hh in range(GROUP):
                cols = pl.ds(pl.multiple_of((g * GROUP + hh) * HEAD_DIM, HEAD_DIM), HEAD_DIM)
                outs[3 + i][:, cols] = m.x_all[g, part_rows(i, hh), :].astype(F32)


    for g in range(groups):
        m.stat_z[g, 0] = jnp.zeros_like(m.stat_z[g, 0])
    meet(
        [(at.b, at.head_peer(s)) for s in range(1, heads)]
        + [at.next(), at.prev()]
        + [at.along_z(s)[1] for s in range(1, at.n_z)]
        + [at.in_plane(s) for s in range(1, plane)]
    )
    text_copies = [
        pltpu.make_async_copy(texts[i], m.text.at[i], m.text_sems.at[i]) for i in range(4)
    ]
    for copy in text_copies:
        copy.start()
    lead = min(LEAD, n)
    pl.loop(0, lead)(send_in)
    for copy in text_copies:
        copy.wait()

    def when_group(t, late, stage):
        past = t - late

        @pl.when((past >= 0) & (past < GROUP * groups) & (lax.rem(past + GROUP * groups, GROUP) == 0))
        def _():
            stage(past // GROUP)

    def when_head(t, late, stage):
        @pl.when((t >= late) & (t < n + late))
        def _():
            stage(t - late)

    def start_stats(g):
        start_all(stats_z, at.n_z, g)

    def late_text(g):
        merge_plane(g)
        pl.loop(0, GROUP)(functools.partial(text_grads, g))
        start_all(scatter_x, at.n_x, g)

    @pl.loop(0, GROUP * (groups - 1) + GROUP + 7)
    def turn(t):
        @pl.when(t + lead < n)
        def _():
            send_in(t + lead)

        when_head(t, 0, keys_in)
        when_group(t, GROUP - 1, start_stats)
        when_group(t, GROUP, merge_z)
        when_head(t, 1, image_grads)
        when_group(t, GROUP + 1, late_text)
        when_group(t, GROUP + 2, sum_x)
        when_head(t, GROUP + 1, finish)
        when_group(t, GROUP + 3, sum_z)
        when_group(t, GROUP + 4, sum_hi)
        when_group(t, GROUP + 5, spread)
        when_group(t, GROUP + 6, write_text)

    @pl.loop(0, n)
    def settle(h):
        for s in range(1, heads):
            for i in range(4):
                arrive(h, i, s).wait_send()
            for i in range(3):
                leave(h, i, s).wait()
        for i in range(3):
            leave_own(h, i).wait()
        for i in range(2):
            halo(h, i).wait_send()
            give_back(h, i).wait_send()

    @pl.loop(0, groups)
    def settle_groups(g):
        for move, count in group_moves:
            for s in range(1, count):
                move(g, s).wait_send()


def body(blocks, heads, img_q, img_k, img_v, img_g, txt_q, txt_k, txt_v, txt_g):
    rows, width = img_q.shape
    txt, wide = txt_q.shape
    in_vmem = pl.BlockSpec(memory_space=pltpu.VMEM)
    anywhere = pl.BlockSpec(memory_space=pltpu.HBM)
    buffers = scratch(blocks, heads, rows, wide, txt)
    out16 = jax.ShapeDtypeStruct((rows, width), BF16)
    text32 = jax.ShapeDtypeStruct((txt, wide), F32)
    return tuple(
        pl.pallas_call(
            functools.partial(kernel, blocks, heads, tuple(buffers)),
            out_shape=[out16] * 3 + [text32] * 3,
            in_specs=[anywhere] * 8,
            out_specs=[anywhere] * 3 + [in_vmem] * 3,
            scratch_shapes=list(buffers.values()),
            compiler_params=pltpu.CompilerParams(
                collective_id=0, has_side_effects=True, vmem_limit_bytes=VMEM_LIMIT
            ),
            name="joint_attention_grads",
        )(img_q, img_k, img_v, img_g, txt_q, txt_k, txt_v, txt_g)
    )


def solution(mesh):
    rows = P(("blk", "head"), None)
    text = P(None, "head")
    return jax.shard_map(
        functools.partial(body, mesh.shape["blk"], mesh.shape["head"]),
        mesh=mesh,
        in_specs=(rows,) * 4 + (text,) * 4,
        out_specs=(rows,) * 3 + (text,) * 3,
        check_vma=False,
    )
```

```python
import functools
import math
from types import SimpleNamespace

import jax
import jax.numpy as jnp
from jax import lax
from jax.experimental import pallas as pl
from jax.experimental.pallas import tpu as pltpu
from jax.sharding import PartitionSpec as P

HEAD_DIM = 128
SCALE = HEAD_DIM ** (-0.5)
EXP2_SCALE = SCALE * math.log2(math.e)
MESH = pl.DeviceIdType.MESH
F32 = jnp.float32
BF16 = jnp.bfloat16
STAT_ROWS = 8
GROUP = 2
LEAD = 2
TILE = 256
VMEM_LIMIT = 50 * 1024 * 1024


def torus_sizes(blocks):
    return {64: (2, 4, 8), 8: (2, 2, 2)}[blocks]


class Place:
    def __init__(self, blocks, heads):
        self.blocks, self.heads = blocks, heads
        self.n_hi, self.n_x, self.n_z = torus_sizes(blocks)
        self.b = lax.axis_index("blk")
        self.c = lax.axis_index("head")
        self.z = lax.rem(self.b, self.n_z)
        self.x = lax.rem(self.b // self.n_z, self.n_x)
        self.hi = self.b // (self.n_z * self.n_x)
        self.part = self.trade(self.hi, self.c)

    def trade(self, hi, c):
        return lax.rem(c + hi * (self.heads // 2), self.heads)

    def device(self, hi, x, z):
        return ((hi * self.n_x + x) * self.n_z + z, self.trade(hi, self.part))

    def shifted(self, by):
        b = lax.rem(self.b + by + self.blocks, self.blocks)
        return (b, self.trade(b // (self.n_z * self.n_x), self.part))

    def next(self):
        return self.shifted(1)

    def prev(self):
        return self.shifted(-1)

    def head_peer(self, step):
        return lax.rem(self.c + step, self.heads)

    def along_z(self, step):
        z = lax.rem(self.z + step, self.n_z)
        return z, self.device(self.hi, self.x, z)

    def along_x(self, step):
        x = lax.rem(self.x + step, self.n_x)
        return x, self.device(self.hi, x, self.z)

    def across(self):
        return self.device(1 - self.hi, self.x, self.z)

    def across_at(self, c):
        return (((1 - self.hi) * self.n_x + self.x) * self.n_z + self.z, c)

    def in_plane(self, step):
        at = lax.rem(self.hi * self.n_x + self.x + step, self.n_hi * self.n_x)
        return self.device(at // self.n_x, lax.rem(at, self.n_x), self.z)


def meet(devices):
    barrier = pltpu.get_barrier_semaphore()
    for device in devices:
        pl.semaphore_signal(barrier, inc=1, device_id=device, device_id_type=MESH)
    pl.semaphore_wait(barrier, len(devices))


def remote(src, dst, sems, slot, device):
    return pltpu.make_async_remote_copy(
        src_ref=src,
        dst_ref=dst,
        send_sem=sems.at[(0,) + slot],
        recv_sem=sems.at[(1,) + slot],
        device_id=device,
        device_id_type=MESH,
    )


def dot_last(left, right):
    return lax.dot_general(
        left, right, (((1,), (1,)), ((), ())), preferred_element_type=F32
    )


def dot_plain(left, right):
    return lax.dot_general(
        left, right, (((1,), (0,)), ((), ())), preferred_element_type=F32
    )


def col_max(array):
    return jnp.max(array, axis=0, keepdims=True)


def col_sum(array):
    return jnp.sum(array, axis=0, keepdims=True)


def merge_stats(parts, per_group):
    rows = [[p[i * per_group : (i + 1) * per_group] for i in range(3)] for p in parts]
    top = functools.reduce(jnp.maximum, [r[0] for r in rows])
    total = jnp.zeros_like(top)
    dots = jnp.zeros_like(top)
    for part_top, part_total, part_dots in rows:
        factor = jnp.exp2(part_top - top)
        total += part_total * factor
        dots += part_dots * factor
    return top, total, dots


def dma(*shape):
    return pltpu.SemaphoreType.DMA(shape)


def scratch(blocks, heads, rows, wide, txt):
    n_hi, n_x, n_z = torus_sizes(blocks)
    plane = n_hi * n_x
    n = wide // HEAD_DIM
    groups = n // GROUP
    block = rows * heads
    sums = 3 * GROUP * txt
    xr = sums // n_x
    zr = xr // n_z
    d = HEAD_DIM
    return dict(
        text=pltpu.VMEM((4, n, txt, d), BF16),
        landed=pltpu.VMEM((4, n, block, d), BF16),
        halo=pltpu.VMEM((2, n, block, d), BF16),
        ready=pltpu.VMEM((3, n, block, d), BF16),
        own=pltpu.VMEM((2, n, block, d), F32),
        give=pltpu.VMEM((2, n, block, d), BF16),
        back=pltpu.VMEM((2, n, block, d), BF16),
        stat_z=pltpu.VMEM((groups, n_z, STAT_ROWS, txt), F32),
        stat_p=pltpu.VMEM((groups, plane, STAT_ROWS, txt), F32),
        stat=pltpu.VMEM((groups, STAT_ROWS, txt), F32),
        part=pltpu.VMEM((groups, sums, d), F32),
        part16=pltpu.VMEM((groups, sums, d), BF16),
        x_in=pltpu.VMEM((groups, n_x - 1, xr, d), BF16),
        x_sum=pltpu.VMEM((groups, xr, d), F32),
        x_sum16=pltpu.VMEM((groups, xr, d), BF16),
        z_in=pltpu.VMEM((groups, n_z - 1, zr, d), BF16),
        hi_in=pltpu.VMEM((groups, 3, zr, d), F32),
        z_all=pltpu.VMEM((groups, xr, d), BF16),
        x_all=pltpu.VMEM((groups, sums, d), BF16),
        text_sems=dma(2, n, 4),
        text_own=dma(n, 4),
        in_sems=dma(2, n, 4, heads),
        in_own=dma(n, 4),
        halo_sems=dma(2, n, 2),
        back_sems=dma(2, n, 2),
        out_sems=dma(2, n, 3, heads),
        out_own=dma(n, 3),
        sz_sems=dma(2, groups, n_z),
        sp_sems=dma(2, groups, plane),
        xs_sems=dma(2, groups, n_x),
        zs_sems=dma(2, groups, n_z),
        hi_sems=dma(2, groups, 3),
        zg_sems=dma(2, groups, n_z),
        xg_sems=dma(2, groups, n_x),
    )


def kernel(blocks, heads, names, *refs):
    ins, outs, rest = refs[:8], refs[8:14], refs[14:]
    images, texts = ins[:4], ins[4:]
    m = SimpleNamespace(**dict(zip(names, rest)))
    at = Place(blocks, heads)
    rows = outs[0].shape[0]
    txt, wide = outs[3].shape
    n = wide // HEAD_DIM
    groups = n // GROUP
    plane = at.n_hi * at.n_x
    xr, zr = m.x_sum.shape[1], m.z_in.shape[2]
    block = rows * heads
    my_rows = pl.ds(at.c * rows, rows)
    first = jnp.where(at.b == 0, 1.0, 0.0).astype(F32)
    last_x, last_z = at.n_x - 1, at.n_z - 1
    corner = ((at.x == 0) & (at.z == 0)) | ((at.x == last_x) & (at.z == last_z))
    relays = ((1, 0, 0), (last_x - 1, last_z, last_x))

    def head_cols(owner, h):
        return pl.ds(pl.multiple_of(owner * wide + h * HEAD_DIM, HEAD_DIM), HEAD_DIM)


    def arrive(h, i, s):
        peer = at.head_peer(s)
        return remote(
            images[i].at[:, head_cols(at.trade(at.hi, peer), h)],
            m.landed.at[i, h, my_rows, :],
            m.in_sems, (h, i, s), (at.b, peer),
        )

    def arrive_own(h, i):
        return pltpu.make_async_copy(
            images[i].at[:, head_cols(at.part, h)],
            m.landed.at[i, h, my_rows, :],
            m.in_own.at[h, i],
        )

    def text_own(h, i):
        return pltpu.make_async_copy(
            texts[i].at[:, head_cols(0, h)], m.text.at[i, h], m.text_own.at[h, i]
        )

    def text_over(h, i):
        return remote(
            texts[i].at[:, head_cols(0, h)], m.text.at[i, h], m.text_sems, (h, i), at.across()
        )

    def text_relay(h, i, to_x):
        return remote(
            m.text.at[i, h], m.text.at[i, h], m.text_sems, (h, i), at.device(1, to_x, at.z)
        )

    def halo(h, i):
        return remote(
            m.landed.at[i + 1, h], m.halo.at[i, h], m.halo_sems, (h, i), at.next()
        )

    def give_back(h, i):
        return remote(m.give.at[i, h], m.back.at[i, h], m.back_sems, (h, i), at.prev())

    def leave(h, i, s):
        peer = at.head_peer(s)
        return remote(
            m.ready.at[i, h, pl.ds(peer * rows, rows), :],
            outs[i].at[:, head_cols(at.part, h)],
            m.out_sems, (h, i, s), (at.b, peer),
        )

    def leave_own(h, i):
        return pltpu.make_async_copy(
            m.ready.at[i, h, my_rows, :],
            outs[i].at[:, head_cols(at.part, h)],
            m.out_own.at[h, i],
        )

    def stats_z(g, s):
        return remote(
            m.stat_z.at[g, 0], m.stat_z.at[g, s], m.sz_sems, (g, s), at.along_z(s)[1]
        )

    def stats_p(g, s):
        return remote(
            m.stat_p.at[g, 0], m.stat_p.at[g, s], m.sp_sems, (g, s), at.in_plane(s)
        )

    def scatter_x(g, s):
        x, device = at.along_x(s)
        return remote(
            m.part16.at[g, pl.ds(x * xr, xr), :], m.x_in.at[g, s - 1],
            m.xs_sems, (g, s), device,
        )

    def scatter_z(g, s):
        z, device = at.along_z(s)
        return remote(
            m.x_sum16.at[g, pl.ds(z * zr, zr), :], m.z_in.at[g, s - 1],
            m.zs_sems, (g, s), device,
        )

    def swap_hi(g, s):
        device = at.across_at(at.part) if s == 1 else (at.b, at.part)
        return remote(m.hi_in.at[g, 0], m.hi_in.at[g, s], m.hi_sems, (g, s), device)

    my_z = pl.ds(at.z * zr, zr)
    my_x = pl.ds(at.x * xr, xr)

    def gather_z(g, s):
        return remote(
            m.z_all.at[g, my_z, :], m.z_all.at[g, my_z, :],
            m.zg_sems, (g, s), at.along_z(s)[1],
        )

    def gather_x(g, s):
        return remote(
            m.z_all.at[g], m.x_all.at[g, my_x, :],
            m.xg_sems, (g, s), at.along_x(s)[1],
        )

    group_moves = [
        (stats_z, at.n_z), (stats_p, plane), (scatter_x, at.n_x), (scatter_z, at.n_z),
        (gather_z, at.n_z), (gather_x, at.n_x),
    ]

    def start_all(move, count, g):
        for s in range(1, count):
            move(g, s).start()

    def await_all(move, count, g):
        for s in range(1, count):
            move(g, s).wait_recv()


    def send_rows(h, arrays):
        for i in arrays:
            for s in (2, 3, 1) if heads == 4 else range(1, heads):
                arrive(h, i, s).start()
            arrive_own(h, i).start()

    def send_in(h):
        @pl.when(h == 0)
        def _():
            send_rows(h, (1, 2))

        @pl.when(h < n - 1)
        def _():
            send_rows(h + 1, (1, 2))

        send_rows(h, (0, 3))

        @pl.when(at.hi == 0)
        def _():
            for i in (1, 0, 2, 3):
                text_own(h, i).start()

        @pl.when((at.hi == 0) & ~corner)
        def _():
            for i in (1, 0, 2, 3):
                text_over(h, i).start()

    def await_text(h):
        @pl.when(at.hi == 0)
        def _():
            for i in range(4):
                text_own(h, i).wait()

        @pl.when(at.hi == 1)
        def _():
            for i in range(4):
                text_over(h, i).wait_recv()

        for x, z, to_x in relays:

            @pl.when((at.hi == 1) & (at.z == z) & (at.x == x))
            def _():
                for i in range(4):
                    text_relay(h, i, to_x).start()

    def await_in(h, i):
        for s in range(1, heads):
            arrive(h, i, s).wait_recv()
        arrive_own(h, i).wait()

    def send_out(h, i):
        for s in (2, 3, 1) if heads == 4 else range(1, heads):
            leave(h, i, s).start()
        leave_own(h, i).start()

    def text_rows(i, h):
        return m.text[i, h]

    def keys_in(h):
        for i in (1, 2):
            await_in(h, i)
            halo(h, i - 1).start()

    def text_stats(h):
        await_text(h)
        g, hh = h // GROUP, lax.rem(h, GROUP)
        query, grad = text_rows(0, h), text_rows(3, h)
        s_img = dot_last(m.landed[1, h], query) * EXP2_SCALE
        s_txt = dot_last(text_rows(1, h), query) * EXP2_SCALE
        top = jnp.maximum(col_max(s_img), col_max(s_txt))
        p_img = jnp.exp2(s_img - top)
        p_txt = jnp.exp2(s_txt - top) * first
        d_img = dot_last(m.landed[2, h], grad)
        d_txt = dot_last(text_rows(2, h), grad)
        m.stat_z[g, 0, pl.ds(hh, 1), :] = top
        m.stat_z[g, 0, pl.ds(GROUP + hh, 1), :] = col_sum(p_img) + col_sum(p_txt)
        m.stat_z[g, 0, pl.ds(2 * GROUP + hh, 1), :] = col_sum(p_img * d_img) + col_sum(
            p_txt * d_txt
        )

    def merge_z(g):
        await_all(stats_z, at.n_z, g)
        merged = merge_stats([m.stat_z[g, s] for s in range(at.n_z)], GROUP)
        m.stat_p[g, 0] = jnp.zeros_like(m.stat_p[g, 0])
        for i in range(3):
            m.stat_p[g, 0, i * GROUP : (i + 1) * GROUP, :] = merged[i]
        start_all(stats_p, plane, g)

    def merge_plane(g):
        await_all(stats_p, plane, g)
        merged = merge_stats([m.stat_p[g, s] for s in range(plane)], GROUP)
        for i in range(3):
            m.stat[g, i * GROUP : (i + 1) * GROUP, :] = merged[i]

    def part_rows(i, hh):
        return pl.ds(pl.multiple_of((i * GROUP + hh) * txt, txt), txt)

    def text_grads(g, hh):
        h = g * GROUP + hh
        query, grad = text_rows(0, h), text_rows(3, h)
        key, value = m.landed[1, h], m.landed[2, h]
        text_key, text_value = text_rows(1, h), text_rows(2, h)
        top = m.stat[g, pl.ds(hh, 1), :]
        total = m.stat[g, pl.ds(GROUP + hh, 1), :]
        inverse = 1.0 / total
        delta = m.stat[g, pl.ds(2 * GROUP + hh, 1), :] * inverse
        w_img = jnp.exp2(dot_last(key, query) * EXP2_SCALE - top) * inverse
        ds_img = (w_img * (dot_last(value, grad) - delta)).astype(BF16)
        w_txt = jnp.exp2(dot_last(text_key, query) * EXP2_SCALE - top) * (inverse * first)
        ds_txt = (w_txt * (dot_last(text_value, grad) - delta)).astype(BF16)
        m.own[0, h] += dot_plain(ds_img, query) * SCALE
        m.own[1, h] += dot_plain(w_img.astype(BF16), grad)
        sums = [
            (dot_plain(key.T, ds_img) + dot_plain(text_key.T, ds_txt)).T * SCALE,
            m.part[g, part_rows(1, hh), :] + dot_plain(ds_txt, query) * SCALE,
            m.part[g, part_rows(2, hh), :] + dot_plain(w_txt.astype(BF16), grad),
        ]
        for i in range(3):
            m.part[g, part_rows(i, hh), :] = sums[i]
            m.part16[g, part_rows(i, hh), :] = sums[i].astype(BF16)

    def image_grads(h):
        for i in (0, 3):
            await_in(h, i)
        for i in range(2):
            halo(h, i).wait_recv()
        g, hh = h // GROUP, lax.rem(h, GROUP)
        keys = [m.landed[1, h], m.halo[0, h], text_rows(1, h)]
        values = [m.landed[2, h], m.halo[1, h], text_rows(2, h)]
        turned = [key.T for key in keys]
        dk_parts, dv_parts = [None] * 3, [None] * 3
        for r in range(0, block, min(block, TILE)):
            these = slice(r, r + min(block, TILE))
            query, grad = m.landed[0, h, these, :], m.landed[3, h, these, :]
            scores = [dot_last(key, query) for key in keys]
            top = functools.reduce(jnp.maximum, [col_max(s) for s in scores]) * EXP2_SCALE
            lifted = [jnp.exp2(s * EXP2_SCALE - top) for s in scores]
            dprobs = [dot_last(value, grad) for value in values]
            inverse = 1.0 / sum(col_sum(p) for p in lifted)
            delta = sum(col_sum(p * d) for p, d in zip(lifted, dprobs)) * inverse
            query_part = None
            for i in range(3):
                weights = lifted[i] * inverse
                dscore = (weights * (dprobs[i] - delta)).astype(BF16)
                dk = dot_plain(dscore, query)
                dv = dot_plain(weights.astype(BF16), grad)
                dk_parts[i] = dk if r == 0 else dk_parts[i] + dk
                dv_parts[i] = dv if r == 0 else dv_parts[i] + dv
                part = dot_plain(turned[i], dscore)
                query_part = part if query_part is None else query_part + part
            m.ready[0, h, these, :] = (query_part.T * SCALE).astype(BF16)
        m.give[0, h] = (dk_parts[1] * SCALE).astype(BF16)
        m.give[1, h] = dv_parts[1].astype(BF16)
        for i in range(2):
            give_back(h, i).start()
        send_out(h, 0)
        m.own[0, h] = dk_parts[0] * SCALE
        m.own[1, h] = dv_parts[0]
        m.part[g, part_rows(1, hh), :] = dk_parts[2] * SCALE
        m.part[g, part_rows(2, hh), :] = dv_parts[2]

    def finish(h):
        for i in range(2):
            give_back(h, i).wait_recv()
            m.ready[i + 1, h] = (m.own[i, h] + m.back[i, h].astype(F32)).astype(BF16)
            send_out(h, i + 1)

    def sum_x(g):
        await_all(scatter_x, at.n_x, g)
        value = m.part[g, my_x, :]
        for s in range(1, at.n_x):
            value = value + m.x_in[g, s - 1].astype(F32)
        m.x_sum[g] = value
        m.x_sum16[g] = value.astype(BF16)
        start_all(scatter_z, at.n_z, g)

    def sum_z(g):
        await_all(scatter_z, at.n_z, g)
        value = m.x_sum[g, my_z, :]
        for s in range(1, at.n_z):
            value = value + m.z_in[g, s - 1].astype(F32)
        m.hi_in[g, 0] = value
        swap_hi(g, 1).start()

        @pl.when(at.hi == 1)
        def _():
            swap_hi(g, 2).start()

    def sum_hi(g):
        swap_hi(g, 1).wait_recv()

        @pl.when(at.hi == 0)
        def _():
            m.z_all[g, my_z, :] = (m.hi_in[g, 0] + m.hi_in[g, 1]).astype(BF16)

        @pl.when(at.hi == 1)
        def _():
            swap_hi(g, 2).wait_recv()
            m.z_all[g, my_z, :] = (m.hi_in[g, 1] + m.hi_in[g, 2]).astype(BF16)

        start_all(gather_z, at.n_z, g)

    def spread(g):
        await_all(gather_z, at.n_z, g)
        m.x_all[g, my_x, :] = m.z_all[g]
        start_all(gather_x, at.n_x, g)

    def write_text(g):
        await_all(gather_x, at.n_x, g)
        for i in range(3):
            for hh in range(GROUP):
                cols = pl.ds(pl.multiple_of((g * GROUP + hh) * HEAD_DIM, HEAD_DIM), HEAD_DIM)
                outs[3 + i][:, cols] = m.x_all[g, part_rows(i, hh), :].astype(F32)


    for g in range(groups):
        m.stat_z[g, 0] = jnp.zeros_like(m.stat_z[g, 0])
    meet(
        [(at.b, at.head_peer(s)) for s in range(1, heads)]
        + [at.next(), at.prev(), at.across_at(at.c)]
        + [at.along_z(s)[1] for s in range(1, at.n_z)]
        + [at.in_plane(s) for s in range(1, plane)]
    )
    lead = min(LEAD, n)
    pl.loop(0, lead)(send_in)

    last = groups - 1

    def in_turn(t, when, stage, g):
        @pl.when(t == when)
        def _():
            stage(g)

    def when_head(t, late, stage):
        @pl.when((t >= late) & (t < n + late))
        def _():
            stage(t - late)

    def start_stats(g):
        start_all(stats_z, at.n_z, g)

    def late_text(g):
        merge_plane(g)
        pl.loop(0, GROUP)(functools.partial(text_grads, g))
        start_all(scatter_x, at.n_x, g)

    train = [sum_x, sum_z, sum_hi, spread, write_text]

    def text_train(t):
        for g in range(groups):
            for k, stage in enumerate(train):
                in_turn(t, (n - 1 if g + 2 <= last and k == 0 else n + (g + 2 > last)) + k, stage, g)

    @pl.loop(0, n + 6)
    def turn(t):
        @pl.when(t + lead < n)
        def _():
            send_in(t + lead)

        when_head(t, 0, keys_in)
        for g in range(groups):
            in_turn(t, GROUP * g + (GROUP if g == last else GROUP + 1), merge_z, g)
        when_head(t, 1, image_grads)
        in_turn(t, n, late_text, last)
        when_head(t, 0, text_stats)
        for g in range(groups):
            in_turn(t, GROUP * g + GROUP - 1, start_stats, g)
        for g in range(last):
            in_turn(t, GROUP * g + GROUP + 1, late_text, g)

        @pl.when(t < n + GROUP)
        def _():
            when_head(t, GROUP + 1, finish)

        text_train(t)

        @pl.when(t >= n + GROUP)
        def _():
            when_head(t, GROUP + 1, finish)

    @pl.loop(0, n)
    def settle(h):
        for s in range(1, heads):
            for i in range(4):
                arrive(h, i, s).wait_send()
            for i in range(3):
                leave(h, i, s).wait()
        for i in range(3):
            leave_own(h, i).wait()
        for i in range(2):
            halo(h, i).wait_send()
            give_back(h, i).wait_send()

        @pl.when((at.hi == 0) & ~corner)
        def _():
            for i in range(4):
                text_over(h, i).wait_send()

        for x, z, to_x in relays:

            @pl.when((at.hi == 1) & (at.z == z) & (at.x == x))
            def _():
                for i in range(4):
                    text_relay(h, i, to_x).wait_send()

    @pl.loop(0, groups)
    def settle_groups(g):
        for move, count in group_moves:
            for s in range(1, count):
                move(g, s).wait_send()
        swap_hi(g, 1).wait_send()

        @pl.when(at.hi == 1)
        def _():
            swap_hi(g, 2).wait_send()


def body(blocks, heads, img_q, img_k, img_v, img_g, txt_q, txt_k, txt_v, txt_g):
    rows, width = img_q.shape
    txt, wide = txt_q.shape
    in_vmem = pl.BlockSpec(memory_space=pltpu.VMEM)
    anywhere = pl.BlockSpec(memory_space=pltpu.HBM)
    buffers = scratch(blocks, heads, rows, wide, txt)
    out16 = jax.ShapeDtypeStruct((rows, width), BF16)
    text32 = jax.ShapeDtypeStruct((txt, wide), F32)
    return tuple(
        pl.pallas_call(
            functools.partial(kernel, blocks, heads, tuple(buffers)),
            out_shape=[out16] * 3 + [text32] * 3,
            in_specs=[anywhere] * 8,
            out_specs=[anywhere] * 3 + [in_vmem] * 3,
            scratch_shapes=list(buffers.values()),
            compiler_params=pltpu.CompilerParams(
                collective_id=0, has_side_effects=True, vmem_limit_bytes=VMEM_LIMIT
            ),
            name="joint_attention_grads",
        )(img_q, img_k, img_v, img_g, txt_q, txt_k, txt_v, txt_g)
    )


def solution(mesh):
    rows = P(("blk", "head"), None)
    text = P(None, "head")
    return jax.shard_map(
        functools.partial(body, mesh.shape["blk"], mesh.shape["head"]),
        mesh=mesh,
        in_specs=(rows,) * 4 + (text,) * 4,
        out_specs=(rows,) * 3 + (text,) * 3,
        check_vma=False,
    )
```

```python
import functools
import math
from types import SimpleNamespace

import jax
import jax.numpy as jnp
from jax import lax
from jax.experimental import pallas as pl
from jax.experimental.pallas import tpu as pltpu
from jax.sharding import PartitionSpec as P

HEAD_DIM = 128
SCALE = HEAD_DIM ** (-0.5)
EXP2_SCALE = SCALE * math.log2(math.e)
MESH = pl.DeviceIdType.MESH
F32 = jnp.float32
BF16 = jnp.bfloat16
STAT_ROWS = 8
GROUPS = 3
AHEAD = 3
TILE = 256
VMEM_LIMIT = 62 * 1024 * 1024


def torus_sizes(blocks):
    return {64: (2, 4, 8), 8: (2, 2, 2)}[blocks]


class Place:
    def __init__(self, blocks, heads):
        self.blocks, self.heads = blocks, heads
        self.n_hi, self.n_x, self.n_z = torus_sizes(blocks)
        self.b = lax.axis_index("blk")
        self.c = lax.axis_index("head")
        self.z = lax.rem(self.b, self.n_z)
        self.x = lax.rem(self.b // self.n_z, self.n_x)
        self.hi = self.b // (self.n_z * self.n_x)
        self.part = self.trade(self.hi, self.c)

    def trade(self, hi, c):
        return lax.rem(c + hi * (self.heads // 2), self.heads)

    def device(self, hi, x, z):
        return ((hi * self.n_x + x) * self.n_z + z, self.trade(hi, self.part))

    def shifted(self, by):
        b = lax.rem(self.b + by + self.blocks, self.blocks)
        return (b, self.trade(b // (self.n_z * self.n_x), self.part))

    def next(self):
        return self.shifted(1)

    def prev(self):
        return self.shifted(-1)

    def head_peer(self, step):
        return lax.rem(self.c + step, self.heads)

    def along_z(self, step):
        z = lax.rem(self.z + step, self.n_z)
        return z, self.device(self.hi, self.x, z)

    def along_x(self, step):
        x = lax.rem(self.x + step, self.n_x)
        return x, self.device(self.hi, x, self.z)

    def across(self):
        return self.device(1 - self.hi, self.x, self.z)

    def across_at(self, c):
        return (((1 - self.hi) * self.n_x + self.x) * self.n_z + self.z, c)

    def in_plane(self, step):
        at = lax.rem(self.hi * self.n_x + self.x + step, self.n_hi * self.n_x)
        return self.device(at // self.n_x, lax.rem(at, self.n_x), self.z)


def meet(devices):
    barrier = pltpu.get_barrier_semaphore()
    for device in devices:
        pl.semaphore_signal(barrier, inc=1, device_id=device, device_id_type=MESH)
    pl.semaphore_wait(barrier, len(devices))


def remote(src, dst, sems, slot, device):
    return pltpu.make_async_remote_copy(
        src_ref=src,
        dst_ref=dst,
        send_sem=sems.at[(0,) + slot],
        recv_sem=sems.at[(1,) + slot],
        device_id=device,
        device_id_type=MESH,
    )


def dot_last(left, right):
    return lax.dot_general(
        left, right, (((1,), (1,)), ((), ())), preferred_element_type=F32
    )


def dot_plain(left, right):
    return lax.dot_general(
        left, right, (((1,), (0,)), ((), ())), preferred_element_type=F32
    )


def col_max(array):
    return jnp.max(array, axis=0, keepdims=True)


def col_sum(array):
    return jnp.sum(array, axis=0, keepdims=True)


def merge_stats(parts):
    rows = [[p[i * STAT_ROWS : (i + 1) * STAT_ROWS] for i in range(3)] for p in parts]
    top = functools.reduce(jnp.maximum, [r[0] for r in rows])
    total = jnp.zeros_like(top)
    dots = jnp.zeros_like(top)
    for part_top, part_total, part_dots in rows:
        factor = jnp.exp2(part_top - top)
        total += part_total * factor
        dots += part_dots * factor
    return jnp.concatenate([top, total, dots], axis=0)


def dma(*shape):
    return pltpu.SemaphoreType.DMA(shape)


def scratch(blocks, heads, rows, wide, txt):
    n_hi, n_x, n_z = torus_sizes(blocks)
    plane = n_hi * n_x
    n = wide // HEAD_DIM
    groups = GROUPS
    block = rows * heads
    sums = n * txt
    xr = sums // n_x
    zr = xr // n_z
    d = HEAD_DIM
    return dict(
        text=pltpu.VMEM((4, n, txt, d), BF16),
        landed=pltpu.VMEM((4, n, block, d), BF16),
        halo=pltpu.VMEM((2, n, block, d), BF16),
        ready=pltpu.VMEM((3, n, block, d), BF16),
        own=pltpu.VMEM((2, n, block, d), F32),
        give=pltpu.VMEM((2, n, block, d), BF16),
        back=pltpu.VMEM((2, n, block, d), BF16),
        stat_z=pltpu.VMEM((1, n_z, 3 * STAT_ROWS, txt), F32),
        stat_p=pltpu.VMEM((1, plane, 3 * STAT_ROWS, txt), F32),
        stat=pltpu.VMEM((3 * STAT_ROWS, txt), F32),
        part=pltpu.VMEM((groups, sums, d), F32),
        part16=pltpu.VMEM((groups, sums, d), BF16),
        selfs=pltpu.VMEM((groups, sums, d), F32),
        x_in=pltpu.VMEM((groups, n_x - 1, xr, d), BF16),
        x_sum=pltpu.VMEM((groups, xr, d), F32),
        x_sum16=pltpu.VMEM((groups, xr, d), BF16),
        z_in=pltpu.VMEM((groups, n_z - 1, zr, d), BF16),
        hi_in=pltpu.VMEM((groups, 3, zr, d), F32),
        z_all=pltpu.VMEM((groups, xr, d), BF16),
        x_all=pltpu.VMEM((groups, sums, d), BF16),
        text_sems=dma(2, n, 4),
        text_own=dma(n, 4),
        in_sems=dma(2, n, 4, heads),
        in_own=dma(n, 4),
        halo_sems=dma(2, n, 2),
        back_sems=dma(2, n, 2),
        out_sems=dma(2, n, 3, heads),
        out_own=dma(n, 3),
        sz_sems=dma(2, 1, n_z),
        sp_sems=dma(2, 1, plane),
        xs_sems=dma(2, groups, n_x),
        zs_sems=dma(2, groups, n_z),
        hi_sems=dma(2, groups, 3),
        zg_sems=dma(2, groups, n_z),
        xg_sems=dma(2, groups, n_x),
    )


def kernel(blocks, heads, names, *refs):
    ins, outs, rest = refs[:8], refs[8:14], refs[14:]
    images, texts = ins[:4], ins[4:]
    m = SimpleNamespace(**dict(zip(names, rest)))
    at = Place(blocks, heads)
    rows = outs[0].shape[0]
    txt, wide = outs[3].shape
    n = wide // HEAD_DIM
    groups = GROUPS
    per = n // 2
    plane = at.n_hi * at.n_x
    xr, zr = m.x_sum.shape[1], m.z_in.shape[2]
    block = rows * heads
    my_rows = pl.ds(at.c * rows, rows)
    once = jnp.where(at.hi == 0, 1.0, 0.0).astype(F32)
    last_x, last_z = at.n_x - 1, at.n_z - 1
    corner = ((at.x == 0) & (at.z == 0)) | ((at.x == last_x) & (at.z == last_z))
    relays = ((1, 0, 0), (last_x - 1, last_z, last_x))

    def head_cols(owner, h):
        return pl.ds(pl.multiple_of(owner * wide + h * HEAD_DIM, HEAD_DIM), HEAD_DIM)


    def arrive(h, i, s):
        peer = at.head_peer(s)
        return remote(
            images[i].at[:, head_cols(at.trade(at.hi, peer), h)],
            m.landed.at[i, h, my_rows, :],
            m.in_sems, (h, i, s), (at.b, peer),
        )

    def arrive_own(h, i):
        return pltpu.make_async_copy(
            images[i].at[:, head_cols(at.part, h)],
            m.landed.at[i, h, my_rows, :],
            m.in_own.at[h, i],
        )

    def text_own(h, i):
        return pltpu.make_async_copy(
            texts[i].at[:, head_cols(0, h)], m.text.at[i, h], m.text_own.at[h, i]
        )

    def text_over(h, i):
        return remote(
            texts[i].at[:, head_cols(0, h)], m.text.at[i, h], m.text_sems, (h, i), at.across()
        )

    def text_relay(h, i, to_x):
        return remote(
            m.text.at[i, h], m.text.at[i, h], m.text_sems, (h, i), at.device(1, to_x, at.z)
        )

    def halo(h, i):
        return remote(
            m.landed.at[i + 1, h], m.halo.at[i, h], m.halo_sems, (h, i), at.next()
        )

    def give_back(h, i):
        return remote(m.give.at[i, h], m.back.at[i, h], m.back_sems, (h, i), at.prev())

    def leave(h, i, s):
        peer = at.head_peer(s)
        return remote(
            m.ready.at[i, h, pl.ds(peer * rows, rows), :],
            outs[i].at[:, head_cols(at.part, h)],
            m.out_sems, (h, i, s), (at.b, peer),
        )

    def leave_own(h, i):
        return pltpu.make_async_copy(
            m.ready.at[i, h, my_rows, :],
            outs[i].at[:, head_cols(at.part, h)],
            m.out_own.at[h, i],
        )

    def stats_z(g, s):
        return remote(
            m.stat_z.at[g, 0], m.stat_z.at[g, s], m.sz_sems, (g, s), at.along_z(s)[1]
        )

    def stats_p(g, s):
        return remote(
            m.stat_p.at[g, 0], m.stat_p.at[g, s], m.sp_sems, (g, s), at.in_plane(s)
        )

    def scatter_x(g, s):
        x, device = at.along_x(s)
        return remote(
            m.part16.at[g, pl.ds(x * xr, xr), :], m.x_in.at[g, s - 1],
            m.xs_sems, (g, s), device,
        )

    def scatter_z(g, s):
        z, device = at.along_z(s)
        return remote(
            m.x_sum16.at[g, pl.ds(z * zr, zr), :], m.z_in.at[g, s - 1],
            m.zs_sems, (g, s), device,
        )

    def swap_hi(g, s):
        device = at.across_at(at.part) if s == 1 else (at.b, at.part)
        return remote(m.hi_in.at[g, 0], m.hi_in.at[g, s], m.hi_sems, (g, s), device)

    my_z = pl.ds(at.z * zr, zr)
    my_x = pl.ds(at.x * xr, xr)

    def gather_z(g, s):
        return remote(
            m.z_all.at[g, my_z, :], m.z_all.at[g, my_z, :],
            m.zg_sems, (g, s), at.along_z(s)[1],
        )

    def gather_x(g, s):
        return remote(
            m.z_all.at[g], m.x_all.at[g, my_x, :],
            m.xg_sems, (g, s), at.along_x(s)[1],
        )

    group_moves = [
        (scatter_x, at.n_x), (scatter_z, at.n_z),
        (gather_z, at.n_z), (gather_x, at.n_x),
    ]

    def start_all(move, count, g):
        for s in range(1, count):
            move(g, s).start()

    def await_all(move, count, g):
        for s in range(1, count):
            move(g, s).wait_recv()


    def send_rows(h, arrays):
        for i in arrays:
            for s in (2, 3, 1) if heads == 4 else range(1, heads):
                arrive(h, i, s).start()
            arrive_own(h, i).start()

    def send_keys(h):
        send_rows(h, (1, 2))
        send_text(h, (0, 3))

        @pl.when(at.hi == 0)
        def _():
            for i in range(4):
                text_own(h, i).start()

    def send_queries(h):
        send_rows(h, (0, 3))
        send_text(h, (1, 2))

    def send_text(h, arrays):
        @pl.when((at.hi == 0) & ~corner)
        def _():
            for i in arrays:
                text_over(h, i).start()

    def await_text(h, arrays):
        @pl.when(at.hi == 1)
        def _():
            for i in arrays:
                text_over(h, i).wait_recv()

        for x, z, to_x in relays:

            @pl.when((at.hi == 1) & (at.z == z) & (at.x == x))
            def _():
                for i in arrays:
                    text_relay(h, i, to_x).start()

    def await_text_own(h):
        @pl.when(at.hi == 0)
        def _():
            for i in range(4):
                text_own(h, i).wait()

    def await_in(h, i):
        for s in range(1, heads):
            arrive(h, i, s).wait_recv()
        arrive_own(h, i).wait()

    def send_out(h, i):
        for s in (2, 3, 1) if heads == 4 else range(1, heads):
            leave(h, i, s).start()
        leave_own(h, i).start()

    def text_rows(i, h):
        return m.text[i, h]

    def keys_in(h):
        for i in (1, 2):
            await_in(h, i)
            halo(h, i - 1).start()

    def text_stats(h):
        await_text_own(h)
        await_text(h, (0, 3))
        query, grad = text_rows(0, h), text_rows(3, h)

        def write(keys, values):
            scores = [dot_last(key, query) * EXP2_SCALE for key in keys]
            top = functools.reduce(jnp.maximum, [col_max(x) for x in scores])
            lifted = [jnp.exp2(x - top) for x in scores]
            dprobs = [dot_last(value, grad) for value in values]
            m.stat_z[0, 0, pl.ds(h, 1), :] = top
            m.stat_z[0, 0, pl.ds(STAT_ROWS + h, 1), :] = sum(col_sum(p) for p in lifted)
            m.stat_z[0, 0, pl.ds(2 * STAT_ROWS + h, 1), :] = sum(
                col_sum(p * d) for p, d in zip(lifted, dprobs)
            )

        @pl.when(at.b == 0)
        def _():
            write((m.landed[1, h], text_rows(1, h)), (m.landed[2, h], text_rows(2, h)))

        @pl.when(at.b != 0)
        def _():
            write((m.landed[1, h],), (m.landed[2, h],))

    def merge_z():
        await_all(stats_z, at.n_z, 0)
        m.stat_p[0, 0] = merge_stats([m.stat_z[0, s] for s in range(at.n_z)])
        start_all(stats_p, plane, 0)

    def merge_plane():
        await_all(stats_p, plane, 0)
        m.stat[...] = merge_stats([m.stat_p[0, s] for s in range(plane)])

    def place(i, h):
        if i == 0:
            g, at_block = groups - 1, h
        else:
            g, at_block = h // per, 2 * lax.rem(h, per) + i - 1
        return g, pl.ds(pl.multiple_of(at_block * txt, txt), txt)

    def text_grads(h):
        query, grad = text_rows(0, h), text_rows(3, h)
        key, value = m.landed[1, h], m.landed[2, h]
        text_key, text_value = text_rows(1, h), text_rows(2, h)
        top = m.stat[pl.ds(h, 1), :]
        total = m.stat[pl.ds(STAT_ROWS + h, 1), :]
        inverse = 1.0 / total
        delta = m.stat[pl.ds(2 * STAT_ROWS + h, 1), :] * inverse
        w_img = jnp.exp2(dot_last(key, query) * EXP2_SCALE - top) * inverse
        ds_img = (w_img * (dot_last(value, grad) - delta)).astype(BF16)
        w_txt = jnp.exp2(dot_last(text_key, query) * EXP2_SCALE - top) * inverse
        ds_txt = (w_txt * (dot_last(text_value, grad) - delta)).astype(BF16)
        m.own[0, h] += dot_plain(ds_img, query) * SCALE
        m.own[1, h] += dot_plain(w_img.astype(BF16), grad)
        sums = dot_plain(key.T, ds_img).T * SCALE
        g, where = place(0, h)
        m.part[g, where, :] = sums
        m.part16[g, where, :] = sums.astype(BF16)
        m.selfs[g, where, :] = dot_plain(text_key.T, ds_txt).T * SCALE
        g, where = place(1, h)
        m.selfs[g, where, :] = dot_plain(ds_txt, query) * SCALE
        g, where = place(2, h)
        m.selfs[g, where, :] = dot_plain(w_txt.astype(BF16), grad)

    def image_grads(h):
        await_text(h, (1, 2))
        for i in (0, 3):
            await_in(h, i)
        for i in range(2):
            halo(h, i).wait_recv()
        keys = [m.landed[1, h], m.halo[0, h], text_rows(1, h)]
        values = [m.landed[2, h], m.halo[1, h], text_rows(2, h)]
        turned = [key.T for key in keys]
        dk_parts, dv_parts = [None] * 3, [None] * 3
        for r in range(0, block, min(block, TILE)):
            these = slice(r, r + min(block, TILE))
            query, grad = m.landed[0, h, these, :], m.landed[3, h, these, :]
            scores = [dot_last(key, query) for key in keys]
            top = functools.reduce(jnp.maximum, [col_max(s) for s in scores]) * EXP2_SCALE
            lifted = [jnp.exp2(s * EXP2_SCALE - top) for s in scores]
            dprobs = [dot_last(value, grad) for value in values]
            inverse = 1.0 / sum(col_sum(p) for p in lifted)
            delta = sum(col_sum(p * d) for p, d in zip(lifted, dprobs)) * inverse
            query_part = None
            for i in range(3):
                weights = lifted[i] * inverse
                dscore = (weights * (dprobs[i] - delta)).astype(BF16)
                dk = dot_plain(dscore, query)
                dv = dot_plain(weights.astype(BF16), grad)
                dk_parts[i] = dk if r == 0 else dk_parts[i] + dk
                dv_parts[i] = dv if r == 0 else dv_parts[i] + dv
                part = dot_plain(turned[i], dscore)
                query_part = part if query_part is None else query_part + part
            m.ready[0, h, these, :] = (query_part.T * SCALE).astype(BF16)
        m.give[0, h] = (dk_parts[1] * SCALE).astype(BF16)
        m.give[1, h] = dv_parts[1].astype(BF16)
        for i in range(2):
            give_back(h, i).start()
        send_out(h, 0)
        m.own[0, h] = dk_parts[0] * SCALE
        m.own[1, h] = dv_parts[0]
        for i, sums in ((1, dk_parts[2] * SCALE), (2, dv_parts[2])):
            g, where = place(i, h)
            m.part[g, where, :] = sums
            m.part16[g, where, :] = sums.astype(BF16)

    def finish(h):
        for i in range(2):
            give_back(h, i).wait_recv()
            m.ready[i + 1, h] = (m.own[i, h] + m.back[i, h].astype(F32)).astype(BF16)
            send_out(h, i + 1)

    def sum_x(g):
        await_all(scatter_x, at.n_x, g)
        value = m.part[g, my_x, :]
        for s in range(1, at.n_x):
            value = value + m.x_in[g, s - 1].astype(F32)
        m.x_sum[g] = value
        m.x_sum16[g] = value.astype(BF16)
        start_all(scatter_z, at.n_z, g)

    def sum_z(g):
        await_all(scatter_z, at.n_z, g)
        value = m.x_sum[g, my_z, :]
        for s in range(1, at.n_z):
            value = value + m.z_in[g, s - 1].astype(F32)
        value = value + m.selfs[g, pl.ds(at.x * xr + at.z * zr, zr), :] * once
        m.hi_in[g, 0] = value
        swap_hi(g, 1).start()

        @pl.when(at.hi == 1)
        def _():
            swap_hi(g, 2).start()

    def sum_hi(g):
        swap_hi(g, 1).wait_recv()

        @pl.when(at.hi == 0)
        def _():
            m.z_all[g, my_z, :] = (m.hi_in[g, 0] + m.hi_in[g, 1]).astype(BF16)

        @pl.when(at.hi == 1)
        def _():
            swap_hi(g, 2).wait_recv()
            m.z_all[g, my_z, :] = (m.hi_in[g, 1] + m.hi_in[g, 2]).astype(BF16)

        start_all(gather_z, at.n_z, g)

    def spread(g):
        await_all(gather_z, at.n_z, g)
        m.x_all[g, my_x, :] = m.z_all[g]
        start_all(gather_x, at.n_x, g)

    def write_text(g):
        await_all(gather_x, at.n_x, g)
        for i in range(3):
            for h in range(n):
                if (groups - 1 if i == 0 else h // per) == g:
                    block_at = (h if i == 0 else 2 * (h % per) + i - 1) * txt
                    outs[3 + i][:, h * HEAD_DIM : (h + 1) * HEAD_DIM] = m.x_all[
                        g, block_at : block_at + txt, :
                    ]


    m.stat_z[0, 0] = jnp.zeros_like(m.stat_z[0, 0])
    meet(
        [(at.b, at.head_peer(s)) for s in range(1, heads)]
        + [at.next(), at.prev(), at.across_at(at.c)]
        + [at.along_z(s)[1] for s in range(1, at.n_z)]
        + [at.in_plane(s) for s in range(1, plane)]
    )
    ahead = min(AHEAD, n - 2)
    pl.loop(0, ahead)(send_keys)

    @pl.loop(0, n)
    def send(h):
        send_queries(h)

        @pl.when(h + ahead < n)
        def _():
            send_keys(h + ahead)

    @pl.loop(0, ahead)
    def begin(h):
        keys_in(h)
        text_stats(h)

    def in_turn(t, when, stage, *args):
        @pl.when(t == when)
        def _():
            stage(*args)

    def start_stats():
        start_all(stats_z, at.n_z, 0)

    def start_sums(g):
        start_all(scatter_x, at.n_x, g)

    def late_text():
        merge_plane()

        @pl.loop(0, n)
        def each(h):
            text_grads(h)

            @pl.when(h < n - 2)
            def _():
                finish(h)

        start_sums(groups - 1)

    train = [sum_x, sum_z, sum_hi, spread, write_text]

    @pl.loop(0, n + 6)
    def turn(t):
        @pl.when(t < n)
        def _():
            image_grads(t)

        in_turn(t, per - 1, start_sums, 0)
        in_turn(t, n - 1, start_sums, 1)

        @pl.when(t + ahead < n)
        def _():
            keys_in(t + ahead)
            text_stats(t + ahead)

        in_turn(t, n - ahead - 1, start_stats)
        in_turn(t, n - 2, merge_z)
        in_turn(t, n - 1, late_text)
        in_turn(t, n - 2, sum_x, 0)
        in_turn(t, n, finish, n - 2)
        for k, stage in enumerate(train):
            for g in reversed(range(groups)):
                if k or g:
                    in_turn(t, n - 1 + k + g, stage, g)
        in_turn(t, n + 1, finish, n - 1)

    @pl.loop(0, n)
    def settle(h):
        for s in range(1, heads):
            for i in range(4):
                arrive(h, i, s).wait_send()
            for i in range(3):
                leave(h, i, s).wait()
        for i in range(3):
            leave_own(h, i).wait()
        for i in range(2):
            halo(h, i).wait_send()
            give_back(h, i).wait_send()

        @pl.when((at.hi == 0) & ~corner)
        def _():
            for i in range(4):
                text_over(h, i).wait_send()

        for x, z, to_x in relays:

            @pl.when((at.hi == 1) & (at.z == z) & (at.x == x))
            def _():
                for i in range(4):
                    text_relay(h, i, to_x).wait_send()

    for move, count in ((stats_z, at.n_z), (stats_p, plane)):
        for s in range(1, count):
            move(0, s).wait_send()

    @pl.loop(0, groups)
    def settle_groups(g):
        for move, count in group_moves:
            for s in range(1, count):
                move(g, s).wait_send()
        swap_hi(g, 1).wait_send()

        @pl.when(at.hi == 1)
        def _():
            swap_hi(g, 2).wait_send()


def body(blocks, heads, img_q, img_k, img_v, img_g, txt_q, txt_k, txt_v, txt_g):
    rows, width = img_q.shape
    txt, wide = txt_q.shape
    in_vmem = pl.BlockSpec(memory_space=pltpu.VMEM)
    anywhere = pl.BlockSpec(memory_space=pltpu.HBM)
    buffers = scratch(blocks, heads, rows, wide, txt)
    out16 = jax.ShapeDtypeStruct((rows, width), BF16)
    text16 = jax.ShapeDtypeStruct((txt, wide), BF16)
    grads = pl.pallas_call(
        functools.partial(kernel, blocks, heads, tuple(buffers)),
        out_shape=[out16] * 3 + [text16] * 3,
        in_specs=[anywhere] * 8,
        out_specs=[anywhere] * 3 + [in_vmem] * 3,
        scratch_shapes=list(buffers.values()),
        compiler_params=pltpu.CompilerParams(
            collective_id=0, has_side_effects=True, vmem_limit_bytes=VMEM_LIMIT
        ),
        name="joint_attention_grads",
    )(img_q, img_k, img_v, img_g, txt_q, txt_k, txt_v, txt_g)
    return (*grads[:3], *(total.astype(F32) for total in grads[3:]))


def solution(mesh):
    rows = P(("blk", "head"), None)
    text = P(None, "head")
    return jax.shard_map(
        functools.partial(body, mesh.shape["blk"], mesh.shape["head"]),
        mesh=mesh,
        in_specs=(rows,) * 4 + (text,) * 4,
        out_specs=(rows,) * 3 + (text,) * 3,
        check_vma=False,
    )
```
